512 devices in a mesh: dp: 16 (over x, y), seq: 32 (over z, core).
Axes of the slice: x: 4, y: 4, z: 16, core: 2. Of those that a mesh axis runs over, the one named last changes fastest.
Arguments:
- queries: bfloat16 [16, 4096, 4096], P('dp', 'seq'), may hold values from -6 to 6
- key_states: bfloat16 [16, 4096, 1024], P('dp', 'seq'), may hold values from -8 to 8
- value_states: bfloat16 [16, 4096, 1024], P('dp', 'seq'), may hold values from -6 to 6
- sink_logit: float32 [32], P('seq'), may hold values from 7 to 12
- out_grad: bfloat16 [16, 4096, 4096], P('dp', 'seq'), may hold values from -16 to 16
- block_table: int32 [32, 32, 8], P('seq'), may hold values from 0 to 31, as said below
Outputs:
- query_grad: bfloat16 [16, 4096, 4096], P('dp', 'seq')
- key_grad: bfloat16 [16, 4096, 1024], P('dp', 'seq')
- value_grad: bfloat16 [16, 4096, 1024], P('dp', 'seq')
- sink_grad: float32 [32], P('seq')
The draws below stay inside these ranges and needn't reach their ends.
Inputs may be any that keep to these rules, and one draw needn't show every extreme that they name: `block_table`: each row lists 8 different key blocks; among them are the query's own block, the two blocks beside it (cyclically) and block 0.
All inputs are finite; a program needn't handle non-finite values.
Results may differ from the reference program's by a relative error of at most 0.0066.
Values may be sent and summed in bfloat16 or wider, within the bound.
No kernel may reach another device: no remote copies, remote signals or barrier semaphores. Data moves between devices by JAX's collectives and lax.ppermute only.
A program may use at most 64 MiB of HBM per device.

```python
import jax
import jax.numpy as jnp
from jax import lax

HEADS = 32
KV_HEADS = 8
HEAD_DIM = 128
BLOCK = 128
KB = 8
SEQS = 16
LEN = 4096
NB = 32


def draw_queries(key, part):
    shape = (SEQS, LEN, HEADS * HEAD_DIM)
    values = jnp.clip(jax.random.normal(jax.random.fold_in(key, 1), shape, jnp.float32), -6.0, 6.0)
    return values.astype(jnp.bfloat16)


def draw_key_states(key, part):
    shape = (SEQS, LEN, KV_HEADS * HEAD_DIM)
    values = jnp.clip(2.5 * jax.random.normal(jax.random.fold_in(key, 2), shape, jnp.float32), -8.0, 8.0)
    return values.astype(jnp.bfloat16)


def draw_out_grad(key, part):
    shape = (SEQS, LEN, HEADS * HEAD_DIM)
    sequence = lax.broadcasted_iota(jnp.int32, (SEQS, 1, 1), 0).astype(jnp.float32)
    factor = 1.0 + 2.0 * sequence / max(SEQS - 1, 1)
    values = jnp.clip(jax.random.normal(jax.random.fold_in(key, 3), shape, jnp.float32), -4.0, 4.0)
    return (values * factor).astype(jnp.bfloat16)


def draw_block_table(key, part):
    rows = lax.broadcasted_iota(jnp.int32, (HEADS, NB, NB), 1)
    columns = lax.broadcasted_iota(jnp.int32, (HEADS, NB, NB), 2)
    noise = jax.random.randint(jax.random.fold_in(key, 4), (HEADS, NB, NB), 0, 2 ** 20, jnp.int32)
    needed = (columns == rows) | (columns == (rows + 1) % NB) | (columns == (rows + NB - 1) % NB) | (columns == 0)
    ranking = noise * NB + columns + jnp.where(needed, 2 ** 30, 0).astype(jnp.int32)
    chosen = lax.top_k(ranking, KB)[1]
    return chosen.astype(jnp.int32)


def levels(stream_key, shape, pieces, low, top_value):
    def one(position, blocks):
        steps = jax.random.uniform(jax.random.fold_in(jax.random.fold_in(stream_key, 6), position), (blocks,), jnp.float32, low / len(pieces), top_value / len(pieces))
        return jnp.repeat(jnp.exp(steps), shape[position] // blocks).reshape((-1,) + (1,) * (len(shape) - position - 1))

    gain = one(*pieces[0])
    for cut in pieces[1:]:
        gain = gain * one(*cut)
    return gain


def gaussian(rng, shape, width, most, split=(), kind=jnp.bfloat16):
    drawn = jax.random.normal(rng, shape, jnp.float32) * width
    if len(split) > 0:
        drawn = levels(rng, shape, split, -0.22, 0.18) * drawn
    return jnp.clip(drawn, min=-most, max=most).astype(kind)


def setup_inputs(seed: int = 0) -> dict:
    key_of = jax.random.split(jax.random.key(seed), 7)
    return {
        "queries": draw_queries(jax.random.fold_in(key_of[6], 71), 0),
        "key_states": draw_key_states(jax.random.fold_in(key_of[6], 71), 0),
        "value_states": gaussian(key_of[2], (SEQS, LEN, KV_HEADS * HEAD_DIM), 1.0, 6.0, ((0, 16), (1, 32))),
        "sink_logit": jnp.clip(7.0 + 5.0 * jax.random.uniform(key_of[3], (HEADS,), jnp.float32) ** levels(key_of[3], (HEADS,), ((0, 32),), -0.2, 0.2), 7.0, 12.0),
        "out_grad": draw_out_grad(jax.random.fold_in(key_of[6], 71), 0),
        "block_table": draw_block_table(jax.random.fold_in(key_of[6], 71), 0),
    }


def head_block(query_head, key_head, value_head, grad_head, sink_value, table):
    scale = HEAD_DIM ** -0.5
    query_blocks = query_head.reshape(NB, BLOCK, HEAD_DIM).astype(jnp.float32)
    key_pick = key_head.reshape(NB, BLOCK, HEAD_DIM)[table].reshape(NB, KB * BLOCK, HEAD_DIM).astype(jnp.float32)
    value_pick = value_head.reshape(NB, BLOCK, HEAD_DIM)[table].reshape(NB, KB * BLOCK, HEAD_DIM).astype(jnp.float32)
    grad_blocks = grad_head.reshape(NB, BLOCK, HEAD_DIM).astype(jnp.float32)
    scores = jnp.einsum('nqd,nkd->nqk', query_blocks, key_pick) * scale
    top = jnp.maximum(jnp.max(scores, -1), sink_value)
    weights = jnp.exp(scores - top[..., None])
    sink_weight = jnp.exp(sink_value - top)
    total = jnp.sum(weights, -1) + sink_weight
    probs = weights / total[..., None]
    sink_prob = sink_weight / total
    probs_low = probs.astype(jnp.bfloat16).astype(jnp.float32)
    attended = jnp.einsum('nqk,nkd->nqd', probs_low, value_pick)
    delta = jnp.sum(grad_blocks * attended, -1)
    dprobs = jnp.einsum('nqd,nkd->nqk', grad_blocks, value_pick)
    dscores = (probs * (dprobs - delta[..., None])).astype(jnp.bfloat16).astype(jnp.float32)
    query_grad = jnp.einsum('nqk,nkd->nqd', dscores, key_pick) * scale
    key_terms = jnp.einsum('nqk,nqd->nkd', dscores, query_blocks) * scale
    value_terms = jnp.einsum('nqk,nqd->nkd', probs_low, grad_blocks)
    flat_table = table.reshape(-1)
    key_grad = jnp.zeros((NB, BLOCK, HEAD_DIM), jnp.float32).at[flat_table].add(key_terms.reshape(NB * KB, BLOCK, HEAD_DIM))
    value_grad = jnp.zeros((NB, BLOCK, HEAD_DIM), jnp.float32).at[flat_table].add(value_terms.reshape(NB * KB, BLOCK, HEAD_DIM))
    sink_grad = -jnp.sum(sink_prob * delta)
    return query_grad.reshape(LEN, HEAD_DIM), key_grad.reshape(LEN, HEAD_DIM), value_grad.reshape(LEN, HEAD_DIM), sink_grad


def reference(queries, key_states, value_states, sink_logit, out_grad, block_table):
    group = HEADS // KV_HEADS

    def per_sequence(items):
        query_seq, key_seq, value_seq, grad_seq = items
        query_heads = query_seq.reshape(LEN, HEADS, HEAD_DIM).transpose(1, 0, 2)
        grad_heads = grad_seq.reshape(LEN, HEADS, HEAD_DIM).transpose(1, 0, 2)
        key_heads = key_seq.reshape(LEN, KV_HEADS, HEAD_DIM).transpose(1, 0, 2)
        value_heads = value_seq.reshape(LEN, KV_HEADS, HEAD_DIM).transpose(1, 0, 2)

        def per_head(head_items):
            query_head, grad_head, sink_value, table, head_index = head_items
            shared = head_index // group
            key_head = lax.dynamic_index_in_dim(key_heads, shared, 0, keepdims=False)
            value_head = lax.dynamic_index_in_dim(value_heads, shared, 0, keepdims=False)
            return head_block(query_head, key_head, value_head, grad_head, sink_value, table)

        query_grads, key_grads, value_grads, sink_grads = lax.map(
            per_head, (query_heads, grad_heads, sink_logit, block_table, jnp.arange(HEADS, dtype=jnp.int32)))
        key_sum = key_grads.reshape(KV_HEADS, group, LEN, HEAD_DIM).sum(1)
        value_sum = value_grads.reshape(KV_HEADS, group, LEN, HEAD_DIM).sum(1)
        return (query_grads.transpose(1, 0, 2).reshape(LEN, HEADS * HEAD_DIM).astype(jnp.bfloat16),
                key_sum.transpose(1, 0, 2).reshape(LEN, KV_HEADS * HEAD_DIM).astype(jnp.bfloat16),
                value_sum.transpose(1, 0, 2).reshape(LEN, KV_HEADS * HEAD_DIM).astype(jnp.bfloat16),
                sink_grads)

    results = lax.map(per_sequence, (queries, key_states, value_states, out_grad))
    return (results[0], results[1], results[2], jnp.sum(results[3], 0))
```

```python
import functools

import jax
import jax.numpy as jnp
from jax import lax
from jax.experimental import pallas as pl
from jax.experimental.pallas import tpu as pltpu
from jax.sharding import PartitionSpec as P

HEADS = 32
KV_HEADS = 8
HEAD_DIM = 128
BLOCK = 128
KB = 8
GROUP = HEADS // KV_HEADS
LOG2E = 1.4426950408889634


def kernel(
    core_ref, table_ref, sink_ref, q0_ref, q1_ref, g0_ref, g1_ref, kv_ref,
    dq0_ref, dq1_ref, dkv_ref, dsink_ref, acc_ref, w_ref,
):
    scale = HEAD_DIM**-0.5
    kv_head = pl.program_id(0)
    acc_ref[...] = jnp.zeros_like(acc_ref)
    w_ref[...] = jnp.zeros_like(w_ref)
    for j in range(GROUP):
        columns = slice(j * HEAD_DIM, (j + 1) * HEAD_DIM)
        sink = sink_ref[pl.ds(kv_head * GROUP + j, 1), :] * LOG2E
        sink_terms = jnp.zeros((1, BLOCK), jnp.float32)
        for s, (q_ref, g_ref, dq_ref) in enumerate(
            ((q0_ref, g0_ref, dq0_ref), (q1_ref, g1_ref, dq1_ref))
        ):
            w_ref[s, :BLOCK, :HEAD_DIM] = q_ref[:, columns]
            w_ref[s, BLOCK:, HEAD_DIM:] = g_ref[:, columns]
            w = w_ref[s]
            rows = []
            for b in range(KB):
                block = table_ref[((kv_head * GROUP + j) * 2 + s) * KB + b]
                rows.append(pl.ds(pl.multiple_of(block * BLOCK, BLOCK), BLOCK))
            both = [
                lax.dot_general(
                    kv_ref[r, :], w, (((1,), (1,)), ((), ())),
                    preferred_element_type=jnp.float32,
                )
                for r in rows
            ]
            scores = [x[:, :BLOCK] * (scale * LOG2E) for x in both]
            dprobs = [x[:, BLOCK:] for x in both]
            top = functools.reduce(jnp.maximum, scores)
            top = jnp.maximum(jnp.max(top, 0, keepdims=True), sink)
            weights = [jnp.exp2(x - top) for x in scores]
            sink_weight = jnp.exp2(sink - top)
            total = jnp.sum(functools.reduce(jnp.add, weights), 0, keepdims=True) + sink_weight
            inverse = 1.0 / total
            probs = [x * inverse for x in weights]
            low = [x.astype(jnp.bfloat16) for x in probs]
            delta = functools.reduce(
                jnp.add, [x.astype(jnp.float32) * y for x, y in zip(low, dprobs)]
            )
            delta = jnp.sum(delta, 0, keepdims=True)
            dscores = [(x * (y - delta)).astype(jnp.bfloat16) for x, y in zip(probs, dprobs)]
            dq = jnp.zeros((BLOCK, HEAD_DIM), jnp.float32)
            for b, r in enumerate(rows):
                terms = jnp.concatenate([dscores[b], low[b]], 1)
                acc_ref[r, :] += jnp.dot(terms, w, preferred_element_type=jnp.float32)
                dq += lax.dot_general(
                    dscores[b], kv_ref[r, :HEAD_DIM], (((0,), (0,)), ((), ())),
                    preferred_element_type=jnp.float32,
                )
            dq_ref[:, columns] = (dq * scale).astype(jnp.bfloat16)
            sink_terms -= sink_weight * inverse * delta
        dsink_ref[pl.ds(kv_head * GROUP + j, 1), :] = sink_terms
    dkv_ref[:, :HEAD_DIM] = (acc_ref[:, :HEAD_DIM] * scale).astype(jnp.bfloat16)
    dkv_ref[:, HEAD_DIM:] = acc_ref[:, HEAD_DIM:].astype(jnp.bfloat16)


def attention(core, table, sink, queries, q_other, grads, g_other, kv):
    length = kv.shape[0]
    kv_heads = KV_HEADS // 2
    wide = GROUP * HEAD_DIM
    own = lambda g, core, table: (0, core[0] * kv_heads + g)
    at = lambda g, core, table: (0, g)
    fixed = lambda g, core, table: (0, 0)
    heads = HEADS // 2
    return pl.pallas_call(
        kernel,
        grid_spec=pltpu.PrefetchScalarGridSpec(
            num_scalar_prefetch=2,
            grid=(kv_heads,),
            in_specs=[
                pl.BlockSpec((heads, BLOCK), fixed),
                pl.BlockSpec((BLOCK, wide), own),
                pl.BlockSpec((BLOCK, wide), at),
                pl.BlockSpec((BLOCK, wide), own),
                pl.BlockSpec((BLOCK, wide), at),
                pl.BlockSpec((length, 2 * HEAD_DIM), at),
            ],
            out_specs=[
                pl.BlockSpec((BLOCK, wide), at),
                pl.BlockSpec((BLOCK, wide), at),
                pl.BlockSpec((length, 2 * HEAD_DIM), at),
                pl.BlockSpec((heads, BLOCK), fixed),
            ],
            scratch_shapes=[
                pltpu.VMEM((length, 2 * HEAD_DIM), jnp.float32),
                pltpu.VMEM((2, 2 * BLOCK, 2 * HEAD_DIM), jnp.bfloat16),
            ],
        ),
        out_shape=[
            jax.ShapeDtypeStruct((BLOCK, kv_heads * wide), jnp.bfloat16),
            jax.ShapeDtypeStruct((BLOCK, kv_heads * wide), jnp.bfloat16),
            jax.ShapeDtypeStruct((length, kv_heads * 2 * HEAD_DIM), jnp.bfloat16),
            jax.ShapeDtypeStruct((heads, BLOCK), jnp.float32),
        ],
        compiler_params=pltpu.CompilerParams(vmem_limit_bytes=48 * 2**20),
        cost_estimate=pl.CostEstimate(
            flops=2 * 5 * heads * 2 * BLOCK * KB * BLOCK * HEAD_DIM,
            bytes_accessed=2 * 2 * length * kv_heads * 2 * HEAD_DIM,
            transcendentals=heads * 2 * BLOCK * KB * BLOCK,
        ),
    )(core, table, sink, queries, q_other, grads, g_other, kv)


def shards(queries, key_states, value_states, sink_logit, out_grad, block_table):
    devices = lax.axis_size("seq")
    chips = devices // 2
    me = lax.axis_index("seq")
    core = me % 2
    half_kv = KV_HEADS // 2
    half = HEADS // 2
    swap = lambda x: lax.ppermute(x, "seq", [(i, i ^ 1) for i in range(devices)])
    groups = [list(range(0, devices, 2)), list(range(1, devices, 2))]

    def halves(x, which, width):
        return lax.dynamic_slice_in_dim(x, which * width, width, axis=1)

    kv = jnp.stack(
        [
            key_states.reshape(BLOCK, KV_HEADS, HEAD_DIM),
            value_states.reshape(BLOCK, KV_HEADS, HEAD_DIM),
        ],
        2,
    ).reshape(BLOCK, KV_HEADS * 2 * HEAD_DIM)
    kv_width = half_kv * 2 * HEAD_DIM
    kv_own = halves(kv, core, kv_width)
    kv_other = swap(halves(kv, 1 - core, kv_width))
    kv_chip = jnp.concatenate([kv_own, kv_other], 0)
    kv_all = lax.all_gather(kv_chip, "seq", axis=0, tiled=True, axis_index_groups=groups)

    q_local = queries.reshape(BLOCK, HEADS * HEAD_DIM)
    g_local = out_grad.reshape(BLOCK, HEADS * HEAD_DIM)
    q_other = swap(halves(q_local, 1 - core, half * HEAD_DIM))
    g_other = swap(halves(g_local, 1 - core, half * HEAD_DIM))

    blocks = block_table.shape[1]
    info = jnp.concatenate(
        [
            block_table.astype(jnp.float32).reshape(blocks, KB),
            jnp.broadcast_to(sink_logit.reshape(1, 1), (blocks, 1)),
        ],
        1,
    ).reshape(chips, 1, 2 * (KB + 1))
    info = jnp.broadcast_to(info, (chips, 2, 2 * (KB + 1))).reshape(devices, 2 * (KB + 1))
    info = lax.all_to_all(info, "seq", split_axis=0, concat_axis=0, tiled=True)
    info = lax.dynamic_slice_in_dim(info, core * half, half, axis=0).reshape(half, 2, KB + 1)
    table = info[:, :, :KB].astype(jnp.int32)
    table = jnp.where(core == 0, table, table[:, ::-1]) ^ core
    sink = jnp.broadcast_to(info[:, 0, KB:], (half, BLOCK))

    dq_own, dq_other, dkv, dsink = attention(
        core.reshape(1).astype(jnp.int32), table.reshape(-1), sink,
        q_local, q_other, g_local, g_other, kv_all,
    )

    dkv_chip = lax.psum_scatter(
        dkv, "seq", scatter_dimension=0, tiled=True, axis_index_groups=groups
    )
    dkv_back = swap(dkv_chip[BLOCK:])
    first = jnp.where(core == 0, dkv_chip[:BLOCK], dkv_back)
    second = jnp.where(core == 0, dkv_back, dkv_chip[:BLOCK])
    dkv_full = jnp.concatenate([first, second], 1).reshape(BLOCK, KV_HEADS, 2, HEAD_DIM)
    key_grad = dkv_full[:, :, 0].reshape(1, BLOCK, KV_HEADS * HEAD_DIM)
    value_grad = dkv_full[:, :, 1].reshape(1, BLOCK, KV_HEADS * HEAD_DIM)

    dq_back = swap(dq_other)
    query_grad = jnp.concatenate(
        [jnp.where(core == 0, dq_own, dq_back), jnp.where(core == 0, dq_back, dq_own)], 1
    ).reshape(1, BLOCK, HEADS * HEAD_DIM)

    total = jnp.sum(dsink, 1).reshape(1, half)
    for step in (1, 2, 4, 8):
        total += lax.ppermute(total, "dp", [(i, i ^ step) for i in range(16)])
    for step in (2, 4, 8, 16):
        total += lax.ppermute(total, "seq", [(i, i ^ step) for i in range(devices)])
    other = swap(total)
    sinks = jnp.concatenate(
        [jnp.where(core == 0, total, other), jnp.where(core == 0, other, total)], 1
    )
    sink_grad = lax.dynamic_slice_in_dim(sinks.reshape(HEADS), me, 1)
    return (query_grad, key_grad, value_grad, sink_grad)


def solution(mesh):
    in_specs = (
        P("dp", "seq", None),
        P("dp", "seq", None),
        P("dp", "seq", None),
        P("seq"),
        P("dp", "seq", None),
        P("seq", None, None),
    )
    out_specs = (P("dp", "seq", None), P("dp", "seq", None), P("dp", "seq", None), P("seq"))
    return jax.shard_map(shards, mesh=mesh, in_specs=in_specs, out_specs=out_specs, check_vma=False)
```

```python
import functools

import jax
import jax.numpy as jnp
from jax import lax
from jax.experimental import pallas as pl
from jax.experimental.pallas import tpu as pltpu
from jax.sharding import PartitionSpec as P

HEADS = 32
KV_HEADS = 8
HEAD_DIM = 128
BLOCK = 128
KB = 8
GROUP = HEADS // KV_HEADS
LOG2E = 1.4426950408889634
SCALE = HEAD_DIM**-0.5
UNROLL = 4


def kernel(
    base, core_ref, table_ref, sink_ref, q0_ref, q1_ref, g0_ref, g1_ref,
    qt0_ref, qt1_ref, gt0_ref, gt1_ref, kv_ref,
    dq0_ref, dq1_ref, dkv_ref, dsink_ref, acc_ref, w_ref, wt_ref, kt_ref,
):
    chips = kv_ref.shape[0]
    local = pl.program_id(0)
    kv_head = base + local
    acc_ref[...] = jnp.zeros_like(acc_ref)
    w_ref[...] = jnp.zeros_like(w_ref)
    wt_ref[...] = jnp.zeros_like(wt_ref)
    for c in range(chips):
        for s in range(2):
            kt_ref[c, s] = kv_ref[c, 0, s * BLOCK : (s + 1) * BLOCK, :].T
    refs = (
        (q0_ref, g0_ref, qt0_ref, gt0_ref, dq0_ref),
        (q1_ref, g1_ref, qt1_ref, gt1_ref, dq1_ref),
    )

    def several(step, _):
        def first(u, s):
            j = step * UNROLL + u
            i = (2 * u + s) % 4
            at = pl.ds(pl.multiple_of(j * HEAD_DIM, HEAD_DIM), HEAD_DIM)
            q_ref, g_ref, qt_ref, gt_ref, _ = refs[s]
            w_ref[i, :BLOCK, :HEAD_DIM] = q_ref[:, at]
            w_ref[i, BLOCK:, HEAD_DIM:] = g_ref[:, at]
            wt_ref[i, :HEAD_DIM, :BLOCK] = qt_ref[at, :]
            wt_ref[i, HEAD_DIM:, BLOCK:] = gt_ref[at, :]
            wt = wt_ref[i]
            places, both = [], []
            for b in range(KB):
                block = table_ref[((kv_head * GROUP + j) * 2 + s) * KB + b]
                chip, slot = block >> 1, block & 1
                rows = pl.ds(pl.multiple_of(slot * BLOCK, BLOCK), BLOCK)
                places.append((chip, slot, rows))
                kv = jnp.concatenate([kv_ref[chip, 0, rows, :], kv_ref[chip, 1, rows, :]], 1)
                both.append(jnp.dot(kv, wt, preferred_element_type=jnp.float32))
            sink = sink_ref[pl.ds(kv_head * GROUP + j, 1), :] * LOG2E
            return at, places, both, sink

        def middle(both, sink):
            scores = [x[:, :BLOCK] for x in both]
            dprobs = [x[:, BLOCK:] for x in both]
            top = jnp.max(functools.reduce(jnp.maximum, scores), 0, keepdims=True)
            top = jnp.maximum(top * (SCALE * LOG2E), sink)
            sink_weight = jnp.exp2(sink - top)
            total = jnp.zeros((BLOCK, BLOCK), jnp.float32)
            delta = jnp.zeros((BLOCK, BLOCK), jnp.float32)
            weights = []
            for x, y in zip(scores, dprobs):
                weight = jnp.exp2(x * (SCALE * LOG2E) - top)
                total += weight
                delta += weight * y
                weights.append(weight)
            inverse = 1.0 / (jnp.sum(total, 0, keepdims=True) + sink_weight)
            delta = jnp.sum(delta, 0, keepdims=True) * inverse
            terms = []
            for x, y in zip(weights, dprobs):
                probs = x * inverse
                dscores = (probs * (y - delta)).astype(jnp.bfloat16)
                terms.append((dscores, probs.astype(jnp.bfloat16)))
            return terms, sink_weight * inverse * delta

        def last(i, s, at, places, terms):
            w = w_ref[i]
            for (chip, _, rows), pair in zip(places, terms):
                acc_ref[chip, rows, :] += jnp.dot(
                    jnp.concatenate(pair, 1), w, preferred_element_type=jnp.float32
                )
            dq = jnp.zeros((HEAD_DIM, BLOCK), jnp.float32)
            for b in range(0, KB, 2):
                (chip0, slot0, _), (chip1, slot1, _) = places[b], places[b + 1]
                kt = jnp.concatenate([kt_ref[chip0, slot0], kt_ref[chip1, slot1]], 1)
                ds = jnp.concatenate([terms[b][0], terms[b + 1][0]], 0)
                dq += jnp.dot(kt, ds, preferred_element_type=jnp.float32)
            refs[s][4][at, :] = (dq * SCALE).astype(jnp.bfloat16)

        count = 2 * UNROLL
        held = first(0, 0)
        sinks = []
        for k in range(count):
            later = first((k + 1) // 2, (k + 1) % 2) if k + 1 < count else None
            at, places, both, sink = held
            terms, sink_term = middle(both, sink)
            sinks.append(sink_term)
            last(k % 4, k % 2, at, places, terms)
            held = later
        for u in range(UNROLL):
            row = pl.ds(local * GROUP + step * UNROLL + u, 1)
            dsink_ref[row, :] = -(sinks[2 * u] + sinks[2 * u + 1])
        return 0

    lax.fori_loop(0, GROUP // UNROLL, several, 0)
    dkv_ref[:, 0] = (acc_ref[:, :, :HEAD_DIM] * SCALE).astype(dkv_ref.dtype)
    dkv_ref[:, 1] = acc_ref[:, :, HEAD_DIM:].astype(dkv_ref.dtype)


def attention(base, kind, core, table, sink, q, q_other, g, g_other, kv):
    chips, heads_here = kv.shape[0], kv.shape[3] // HEAD_DIM
    kv_heads = KV_HEADS // 2
    wide = GROUP * HEAD_DIM
    half = HEADS // 2
    fixed = lambda i, core, table: (0, 0)
    big = pl.BlockSpec((chips, 2, 2 * BLOCK, HEAD_DIM), lambda i, core, table: (0, 0, 0, i))
    own = pl.BlockSpec((BLOCK, wide), lambda i, core, table: (0, core[0] * kv_heads + base + i))
    other = pl.BlockSpec((BLOCK, wide), lambda i, core, table: (0, base + i))
    own_t = pl.BlockSpec((wide, BLOCK), lambda i, core, table: (core[0] * kv_heads + base + i, 0))
    other_t = pl.BlockSpec((wide, BLOCK), lambda i, core, table: (base + i, 0))
    out_t = pl.BlockSpec((wide, BLOCK), lambda i, core, table: (i, 0))
    pairs = heads_here * GROUP * 2
    return pl.pallas_call(
        functools.partial(kernel, base),
        grid_spec=pltpu.PrefetchScalarGridSpec(
            num_scalar_prefetch=2,
            grid=(heads_here,),
            in_specs=[
                pl.BlockSpec((half, BLOCK), fixed),
                own, other, own, other, own_t, other_t, own_t, other_t, big,
            ],
            out_specs=[out_t, out_t, big, pl.BlockSpec((heads_here * GROUP, BLOCK), fixed)],
            scratch_shapes=[
                pltpu.VMEM((chips, 2 * BLOCK, 2 * HEAD_DIM), jnp.float32),
                pltpu.VMEM((4, 2 * BLOCK, 2 * HEAD_DIM), jnp.bfloat16),
                pltpu.VMEM((4, 2 * HEAD_DIM, 2 * BLOCK), jnp.bfloat16),
                pltpu.VMEM((chips, 2, HEAD_DIM, BLOCK), jnp.bfloat16),
            ],
        ),
        out_shape=[
            jax.ShapeDtypeStruct((heads_here * wide, BLOCK), jnp.bfloat16),
            jax.ShapeDtypeStruct((heads_here * wide, BLOCK), jnp.bfloat16),
            jax.ShapeDtypeStruct((chips, 2, 2 * BLOCK, heads_here * HEAD_DIM), kind),
            jax.ShapeDtypeStruct((heads_here * GROUP, BLOCK), jnp.float32),
        ],
        compiler_params=pltpu.CompilerParams(vmem_limit_bytes=58 * 2**20),
        cost_estimate=pl.CostEstimate(
            flops=2 * 10 * pairs * BLOCK * KB * BLOCK * HEAD_DIM,
            bytes_accessed=2 * 2 * chips * 2 * 2 * BLOCK * heads_here * HEAD_DIM,
            transcendentals=pairs * BLOCK * KB * BLOCK,
        ),
    )(core, table, sink, q, q_other, g, g_other, q.T, q_other.T, g.T, g_other.T, kv)


def shards(queries, key_states, value_states, sink_logit, out_grad, block_table):
    devices = lax.axis_size("seq")
    chips = devices // 2
    me = lax.axis_index("seq")
    chip, core = me // 2, me % 2
    half = HEADS // 2
    half_kv = KV_HEADS // 2
    width = half_kv * HEAD_DIM
    swap = lambda x: lax.ppermute(x, "seq", [(i, i ^ 1) for i in range(devices)])
    groups = [list(range(0, devices, 2)), list(range(1, devices, 2))]
    cut = lambda x, which, size: lax.dynamic_slice_in_dim(x, which * size, size, axis=x.ndim - 1)
    order = lambda mine, theirs: jnp.concatenate(
        [jnp.where(core == 0, mine, theirs), jnp.where(core == 0, theirs, mine)], -1
    )

    kv = jnp.stack([key_states[0], value_states[0]], 0)
    kv_chip = jnp.concatenate([cut(kv, core, width), swap(cut(kv, 1 - core, width))], 1)[None]
    kv_all = lax.all_gather(kv_chip, "seq", axis=0, tiled=True, axis_index_groups=groups)
    q_local, g_local = queries[0], out_grad[0]
    q_other = swap(cut(q_local, 1 - core, half * HEAD_DIM))
    g_other = swap(cut(g_local, 1 - core, half * HEAD_DIM))

    blocks = block_table.shape[1]
    info = jnp.concatenate(
        [
            block_table.astype(jnp.float32).reshape(blocks, KB),
            jnp.broadcast_to(sink_logit.reshape(1, 1), (blocks, 1)),
        ],
        1,
    ).reshape(chips, 1, 2 * (KB + 1))
    info = jnp.broadcast_to(info, (chips, 2, 2 * (KB + 1))).reshape(devices, 2 * (KB + 1))
    info = lax.all_to_all(info, "seq", split_axis=0, concat_axis=0, tiled=True)
    info = lax.dynamic_slice_in_dim(info, core * half, half, axis=0).reshape(half, 2, KB + 1)
    table = info[:, :, :KB].astype(jnp.int32)
    table = jnp.where(core == 0, table, table[:, ::-1]) ^ core
    sink = jnp.broadcast_to(info[:, 0, KB:], (half, BLOCK))
    core_at = core.reshape(1).astype(jnp.int32)
    local = (q_local, q_other, g_local, g_other)
    dq_own, dq_other, dkv, dsink = attention(
        0, jnp.bfloat16, core_at, table.reshape(-1), sink, *local, kv_all
    )
    dkv_chip = lax.psum_scatter(
        dkv, "seq", scatter_dimension=0, tiled=True, axis_index_groups=groups
    )[0]
    sides = (dkv_chip[:, :BLOCK], swap(dkv_chip[:, BLOCK:]))
    key_grad = order(*[x[0] for x in sides])[None]
    value_grad = order(*[x[1] for x in sides])[None]

    query_grad = order(dq_own.T, swap(dq_other).T)[None]

    total = jnp.sum(dsink, 1).reshape(1, half)
    for step in (1, 2, 4, 8):
        total += lax.ppermute(total, "dp", [(i, i ^ step) for i in range(16)])
    for step in (2, 4, 8, 16):
        total += lax.ppermute(total, "seq", [(i, i ^ step) for i in range(devices)])
    sinks = order(total, swap(total)).reshape(HEADS)
    sink_grad = lax.dynamic_slice_in_dim(sinks, me, 1)
    return (query_grad, key_grad, value_grad, sink_grad)


def solution(mesh):
    in_specs = (
        P("dp", "seq", None),
        P("dp", "seq", None),
        P("dp", "seq", None),
        P("seq"),
        P("dp", "seq", None),
        P("seq", None, None),
    )
    out_specs = (P("dp", "seq", None), P("dp", "seq", None), P("dp", "seq", None), P("seq"))
    return jax.shard_map(shards, mesh=mesh, in_specs=in_specs, out_specs=out_specs, check_vma=False)
```

```python
import functools

import jax
import jax.numpy as jnp
from jax import lax
from jax.experimental import pallas as pl
from jax.experimental.pallas import tpu as pltpu
from jax.sharding import PartitionSpec as P

HEADS = 32
KV_HEADS = 8
HEAD_DIM = 128
BLOCK = 128
KB = 8
GROUP = HEADS // KV_HEADS
LOG2E = 1.4426950408889634
SCALE = HEAD_DIM**-0.5
UNROLL = 4


def kernel(
    core_ref, table_ref, sink_ref, q0_ref, q1_ref, g0_ref, g1_ref,
    qt0_ref, qt1_ref, gt0_ref, gt1_ref, k_ref, v_ref,
    dq0_ref, dq1_ref, dkv_ref, dsink_ref, acc_ref, w_ref, wt_ref, kt_ref,
):
    kv_head = pl.program_id(0)
    acc_ref[...] = jnp.zeros_like(acc_ref)
    w_ref[...] = jnp.zeros_like(w_ref)
    wt_ref[...] = jnp.zeros_like(wt_ref)
    for c in range(k_ref.shape[0]):
        kt_ref[c] = k_ref[c].T
    refs = (
        (q0_ref, g0_ref, qt0_ref, gt0_ref, dq0_ref),
        (q1_ref, g1_ref, qt1_ref, gt1_ref, dq1_ref),
    )

    def several(step, _):
        def first(u, s):
            j = step * UNROLL + u
            i = (2 * u + s) % 4
            at = pl.ds(pl.multiple_of(j * HEAD_DIM, HEAD_DIM), HEAD_DIM)
            q_ref, g_ref, qt_ref, gt_ref, _ = refs[s]
            w_ref[i, :BLOCK, :HEAD_DIM] = q_ref[:, at]
            w_ref[i, BLOCK:, HEAD_DIM:] = g_ref[:, at]
            wt_ref[i, :HEAD_DIM, :BLOCK] = qt_ref[at, :]
            wt_ref[i, HEAD_DIM:, BLOCK:] = gt_ref[at, :]
            wt = wt_ref[i]
            places, both = [], []
            for b in range(KB):
                block = table_ref[((kv_head * GROUP + j) * 2 + s) * KB + b]
                place = block ^ core_ref[0]
                rows = pl.ds(pl.multiple_of((place & 1) * BLOCK, BLOCK), BLOCK)
                places.append((block, place >> 1, rows))
                kv = jnp.concatenate([k_ref[block], v_ref[block]], 1)
                both.append(jnp.dot(kv, wt, preferred_element_type=jnp.float32))
            sink = sink_ref[kv_head * GROUP + j] * LOG2E
            return at, places, both, sink

        def middle(both, sink):
            scores = [x[:, :BLOCK] for x in both]
            dprobs = [x[:, BLOCK:] for x in both]
            top = jnp.max(functools.reduce(jnp.maximum, scores), 0, keepdims=True)
            top = jnp.maximum(top * (SCALE * LOG2E), sink)
            sink_weight = jnp.exp2(sink - top)
            total = jnp.zeros((BLOCK, BLOCK), jnp.float32)
            delta = jnp.zeros((BLOCK, BLOCK), jnp.float32)
            weights = []
            for x, y in zip(scores, dprobs):
                weight = jnp.exp2(x * (SCALE * LOG2E) - top)
                total += weight
                delta += weight * y
                weights.append(weight)
            inverse = 1.0 / (jnp.sum(total, 0, keepdims=True) + sink_weight)
            delta = jnp.sum(delta, 0, keepdims=True) * inverse
            terms = []
            for x, y in zip(weights, dprobs):
                probs = x * inverse
                dscores = (probs * (y - delta)).astype(jnp.bfloat16)
                terms.append((dscores, probs.astype(jnp.bfloat16)))
            return terms, sink_weight * inverse * delta

        def last(i, s, at, places, terms):
            w = w_ref[i]
            for (_, chip, rows), pair in zip(places, terms):
                acc_ref[chip, rows, :] += jnp.dot(
                    jnp.concatenate(pair, 1), w, preferred_element_type=jnp.float32
                )
            dq = jnp.zeros((HEAD_DIM, BLOCK), jnp.float32)
            for b in range(0, KB, 2):
                kt = jnp.concatenate([kt_ref[places[b][0]], kt_ref[places[b + 1][0]]], 1)
                ds = jnp.concatenate([terms[b][0], terms[b + 1][0]], 0)
                dq += jnp.dot(kt, ds, preferred_element_type=jnp.float32)
            refs[s][4][at, :] = (dq * SCALE).astype(jnp.bfloat16)

        count = 2 * UNROLL
        held = first(0, 0)
        sinks = []
        for k in range(count):
            later = first((k + 1) // 2, (k + 1) % 2) if k + 1 < count else None
            at, places, both, sink = held
            terms, sink_term = middle(both, sink)
            sinks.append(sink_term)
            last(k % 4, k % 2, at, places, terms)
            held = later
        for u in range(UNROLL):
            row = pl.ds(kv_head * GROUP + step * UNROLL + u, 1)
            dsink_ref[row, :] = -(sinks[2 * u] + sinks[2 * u + 1])
        return 0

    lax.fori_loop(0, GROUP // UNROLL, several, 0)
    dkv_ref[:, 0] = (acc_ref[:, :, :HEAD_DIM] * SCALE).astype(dkv_ref.dtype)
    dkv_ref[:, 1] = acc_ref[:, :, HEAD_DIM:].astype(dkv_ref.dtype)


def attention(core, table, sink, q, q_other, g, g_other, kv):
    blocks = kv.shape[0]
    chips = blocks // 2
    kv_heads = KV_HEADS // 2
    wide = GROUP * HEAD_DIM
    half = HEADS // 2
    fixed = lambda i, core, table, sink: (0, 0)
    keys = pl.BlockSpec(
        (blocks, BLOCK, HEAD_DIM), lambda i, core, table, sink: (0, 0, core[0] * kv_heads + i)
    )
    values = pl.BlockSpec(
        (blocks, BLOCK, HEAD_DIM),
        lambda i, core, table, sink: (0, 0, KV_HEADS + core[0] * kv_heads + i),
    )
    big = pl.BlockSpec((chips, 2, 2 * BLOCK, HEAD_DIM), lambda i, core, table, sink: (0, 0, 0, i))
    own = pl.BlockSpec((BLOCK, wide), lambda i, core, table, sink: (0, core[0] * kv_heads + i))
    other = pl.BlockSpec((BLOCK, wide), lambda i, core, table, sink: (0, i))
    own_t = pl.BlockSpec((wide, BLOCK), lambda i, core, table, sink: (core[0] * kv_heads + i, 0))
    other_t = pl.BlockSpec((wide, BLOCK), lambda i, core, table, sink: (i, 0))
    out_t = pl.BlockSpec((wide, BLOCK), lambda i, core, table, sink: (i, 0))
    pairs = kv_heads * GROUP * 2
    return pl.pallas_call(
        kernel,
        grid_spec=pltpu.PrefetchScalarGridSpec(
            num_scalar_prefetch=3,
            grid=(kv_heads,),
            in_specs=[
                own, other, own, other, own_t, other_t, own_t, other_t, keys, values,
            ],
            out_specs=[out_t, out_t, big, pl.BlockSpec((kv_heads * GROUP, BLOCK), fixed)],
            scratch_shapes=[
                pltpu.VMEM((chips, 2 * BLOCK, 2 * HEAD_DIM), jnp.float32),
                pltpu.VMEM((4, 2 * BLOCK, 2 * HEAD_DIM), jnp.bfloat16),
                pltpu.VMEM((4, 2 * HEAD_DIM, 2 * BLOCK), jnp.bfloat16),
                pltpu.VMEM((blocks, HEAD_DIM, BLOCK), jnp.bfloat16),
            ],
        ),
        out_shape=[
            jax.ShapeDtypeStruct((kv_heads * wide, BLOCK), jnp.bfloat16),
            jax.ShapeDtypeStruct((kv_heads * wide, BLOCK), jnp.bfloat16),
            jax.ShapeDtypeStruct((chips, 2, 2 * BLOCK, kv_heads * HEAD_DIM), jnp.bfloat16),
            jax.ShapeDtypeStruct((kv_heads * GROUP, BLOCK), jnp.float32),
        ],
        compiler_params=pltpu.CompilerParams(vmem_limit_bytes=58 * 2**20),
        cost_estimate=pl.CostEstimate(
            flops=2 * 10 * pairs * BLOCK * KB * BLOCK * HEAD_DIM,
            bytes_accessed=2 * 2 * chips * 2 * 2 * BLOCK * kv_heads * HEAD_DIM,
            transcendentals=pairs * BLOCK * KB * BLOCK,
        ),
    )(core, table, sink, q, q_other, g, g_other, q.T, q_other.T, g.T, g_other.T, kv, kv)


def shards(queries, key_states, value_states, sink_logit, out_grad, block_table):
    devices = lax.axis_size("seq")
    chips = devices // 2
    me = lax.axis_index("seq")
    chip, core = me // 2, me % 2
    half = HEADS // 2
    swap = lambda x: lax.ppermute(x, "seq", [(i, i ^ 1) for i in range(devices)])
    groups = [list(range(0, devices, 2)), list(range(1, devices, 2))]
    cut = lambda x, which, size: lax.dynamic_slice_in_dim(x, which * size, size, axis=x.ndim - 1)
    order = lambda mine, theirs: jnp.concatenate(
        [jnp.where(core == 0, mine, theirs), jnp.where(core == 0, theirs, mine)], -1
    )

    kv_all = lax.all_gather(jnp.concatenate([key_states, value_states], 2), "seq", axis=0, tiled=True)

    q_local, g_local = queries[0], out_grad[0]
    q_other = swap(cut(q_local, 1 - core, half * HEAD_DIM))
    g_other = swap(cut(g_local, 1 - core, half * HEAD_DIM))

    blocks = block_table.shape[1]
    info = jnp.concatenate(
        [
            block_table.astype(jnp.float32).reshape(blocks, KB),
            jnp.broadcast_to(sink_logit.reshape(1, 1), (blocks, 1)),
        ],
        1,
    ).reshape(chips, 1, 2 * (KB + 1))
    info = jnp.broadcast_to(info, (chips, 2, 2 * (KB + 1))).reshape(devices, 2 * (KB + 1))
    info = lax.all_to_all(info, "seq", split_axis=0, concat_axis=0, tiled=True)
    info = lax.dynamic_slice_in_dim(info, core * half, half, axis=0).reshape(half, 2, KB + 1)
    table = info[:, :, :KB].astype(jnp.int32)
    table = jnp.where(core == 0, table, table[:, ::-1])
    sink = info[:, 0, KB]
    core_at = core.reshape(1).astype(jnp.int32)
    local = (q_local, q_other, g_local, g_other)
    dq_own, dq_other, dkv, dsink = attention(
        core_at, table.reshape(-1), sink, *local, kv_all
    )
    dkv_chip = lax.psum_scatter(
        dkv, "seq", scatter_dimension=0, tiled=True, axis_index_groups=groups
    )[0]
    sides = (dkv_chip[:, :BLOCK], swap(dkv_chip[:, BLOCK:]))
    key_grad = order(*[x[0] for x in sides])[None]
    value_grad = order(*[x[1] for x in sides])[None]

    query_grad = order(dq_own.T, swap(dq_other).T)[None]

    total = jnp.sum(dsink, 1).reshape(1, half)
    for step in (1, 2, 4, 8):
        total += lax.ppermute(total, "dp", [(i, i ^ step) for i in range(16)])
    for step in (2, 4, 8, 16):
        total += lax.ppermute(total, "seq", [(i, i ^ step) for i in range(devices)])
    sinks = order(total, swap(total)).reshape(HEADS)
    sink_grad = lax.dynamic_slice_in_dim(sinks, me, 1)
    return (query_grad, key_grad, value_grad, sink_grad)


def solution(mesh):
    in_specs = (
        P("dp", "seq", None),
        P("dp", "seq", None),
        P("dp", "seq", None),
        P("seq"),
        P("dp", "seq", None),
        P("seq", None, None),
    )
    out_specs = (P("dp", "seq", None), P("dp", "seq", None), P("dp", "seq", None), P("seq"))
    return jax.shard_map(shards, mesh=mesh, in_specs=in_specs, out_specs=out_specs, check_vma=False)
```

```python
import functools

import jax
import jax.numpy as jnp
from jax import lax
from jax.experimental import pallas as pl
from jax.experimental.pallas import tpu as pltpu
from jax.sharding import PartitionSpec as P

HEADS = 32
KV_HEADS = 8
HEAD_DIM = 128
BLOCK = 128
KB = 8
GROUP = HEADS // KV_HEADS
LOG2E = 1.4426950408889634
SCALE = HEAD_DIM**-0.5
UNROLL = 4


def kernel(
    core_ref, table_ref, sink_ref, q0_ref, q1_ref, g0_ref, g1_ref,
    qt0_ref, qt1_ref, gt0_ref, gt1_ref, k_ref, v_ref,
    dq0_ref, dq1_ref, dkv_ref, dsink_ref, acc_ref, w_ref, wt_ref, kt_ref,
):
    kv_head = pl.program_id(0)
    acc_ref[...] = jnp.zeros_like(acc_ref)
    w_ref[...] = jnp.zeros_like(w_ref)
    wt_ref[...] = jnp.zeros_like(wt_ref)
    for c in range(k_ref.shape[0]):
        kt_ref[c] = k_ref[c].T
    refs = (
        (q0_ref, g0_ref, qt0_ref, gt0_ref, dq0_ref),
        (q1_ref, g1_ref, qt1_ref, gt1_ref, dq1_ref),
    )

    def several(step, _):
        def first(u, s):
            j = step * UNROLL + u
            i = (2 * u + s) % 4
            at = pl.ds(pl.multiple_of(j * HEAD_DIM, HEAD_DIM), HEAD_DIM)
            q_ref, g_ref, qt_ref, gt_ref, _ = refs[s]
            w_ref[i, :BLOCK, :HEAD_DIM] = q_ref[:, at]
            w_ref[i, BLOCK:, HEAD_DIM:] = g_ref[:, at]
            wt_ref[i, :HEAD_DIM, :BLOCK] = qt_ref[at, :]
            wt_ref[i, HEAD_DIM:, BLOCK:] = gt_ref[at, :]
            wt = wt_ref[i]
            places, both = [], []
            for b in range(KB):
                block = table_ref[((kv_head * GROUP + j) * 2 + s) * KB + b]
                place = block ^ core_ref[0]
                rows = pl.ds(pl.multiple_of((place & 1) * BLOCK, BLOCK), BLOCK)
                places.append((block, place >> 1, rows))
                kv = jnp.concatenate([k_ref[block], v_ref[block]], 1)
                both.append(jnp.dot(kv, wt, preferred_element_type=jnp.float32))
            sink = sink_ref[kv_head * GROUP + j] * LOG2E
            return at, places, both, sink

        def middle(both, sink):
            scores = [x[:, :BLOCK] for x in both]
            dprobs = [x[:, BLOCK:] for x in both]
            top = jnp.max(functools.reduce(jnp.maximum, scores), 0, keepdims=True)
            top = jnp.maximum(top * (SCALE * LOG2E), sink)
            sink_weight = jnp.exp2(sink - top)
            total = jnp.zeros((BLOCK, BLOCK), jnp.float32)
            delta = jnp.zeros((BLOCK, BLOCK), jnp.float32)
            weights = []
            for x, y in zip(scores, dprobs):
                weight = jnp.exp2(x * (SCALE * LOG2E) - top)
                total += weight
                delta += weight * y
                weights.append(weight)
            inverse = 1.0 / (jnp.sum(total, 0, keepdims=True) + sink_weight)
            delta = jnp.sum(delta, 0, keepdims=True) * inverse
            terms = []
            for x, y in zip(weights, dprobs):
                probs = x * inverse
                dscores = (probs * (y - delta)).astype(jnp.bfloat16)
                terms.append((dscores, probs.astype(jnp.bfloat16)))
            return terms, sink_weight * inverse * delta

        def last(i, s, at, places, terms):
            w = w_ref[i]
            for (_, chip, rows), pair in zip(places, terms):
                acc_ref[chip, rows, :] += jnp.dot(
                    jnp.concatenate(pair, 1), w, preferred_element_type=jnp.float32
                )
            dq = jnp.zeros((HEAD_DIM, BLOCK), jnp.float32)
            for b in range(0, KB, 2):
                kt = jnp.concatenate([kt_ref[places[b][0]], kt_ref[places[b + 1][0]]], 1)
                ds = jnp.concatenate([terms[b][0], terms[b + 1][0]], 0)
                dq += jnp.dot(kt, ds, preferred_element_type=jnp.float32)
            refs[s][4][at, :] = (dq * SCALE).astype(jnp.bfloat16)

        count = 2 * UNROLL
        held = first(0, 0)
        next1 = first(0, 1)
        sinks = []
        for k in range(count):
            later = first((k + 2) // 2, (k + 2) % 2) if k + 2 < count else None
            at, places, both, sink = held
            terms, sink_term = middle(both, sink)
            sinks.append(sink_term)
            last(k % 4, k % 2, at, places, terms)
            held, next1 = next1, later
        for u in range(UNROLL):
            row = pl.ds(kv_head * GROUP + step * UNROLL + u, 1)
            dsink_ref[row, :] = -(sinks[2 * u] + sinks[2 * u + 1])
        return 0

    lax.fori_loop(0, GROUP // UNROLL, several, 0)
    dkv_ref[:, 0] = (acc_ref[:, :, :HEAD_DIM] * SCALE).astype(dkv_ref.dtype)
    dkv_ref[:, 1] = acc_ref[:, :, HEAD_DIM:].astype(dkv_ref.dtype)


def attention(core, table, sink, q, q_other, g, g_other, kv):
    blocks = kv.shape[0]
    chips = blocks // 2
    kv_heads = KV_HEADS // 2
    wide = GROUP * HEAD_DIM
    half = HEADS // 2
    fixed = lambda i, core, table, sink: (0, 0)
    keys = pl.BlockSpec(
        (blocks, BLOCK, HEAD_DIM), lambda i, core, table, sink: (0, 0, core[0] * kv_heads + i)
    )
    values = pl.BlockSpec(
        (blocks, BLOCK, HEAD_DIM),
        lambda i, core, table, sink: (0, 0, KV_HEADS + core[0] * kv_heads + i),
    )
    big = pl.BlockSpec((chips, 2, 2 * BLOCK, HEAD_DIM), lambda i, core, table, sink: (0, 0, 0, i))
    own = pl.BlockSpec((BLOCK, wide), lambda i, core, table, sink: (0, core[0] * kv_heads + i))
    other = pl.BlockSpec((BLOCK, wide), lambda i, core, table, sink: (0, i))
    own_t = pl.BlockSpec((wide, BLOCK), lambda i, core, table, sink: (core[0] * kv_heads + i, 0))
    other_t = pl.BlockSpec((wide, BLOCK), lambda i, core, table, sink: (i, 0))
    out_t = pl.BlockSpec((wide, BLOCK), lambda i, core, table, sink: (i, 0))
    pairs = kv_heads * GROUP * 2
    return pl.pallas_call(
        kernel,
        grid_spec=pltpu.PrefetchScalarGridSpec(
            num_scalar_prefetch=3,
            grid=(kv_heads,),
            in_specs=[
                own, other, own, other, own_t, other_t, own_t, other_t, keys, values,
            ],
            out_specs=[out_t, out_t, big, pl.BlockSpec((kv_heads * GROUP, BLOCK), fixed)],
            scratch_shapes=[
                pltpu.VMEM((chips, 2 * BLOCK, 2 * HEAD_DIM), jnp.float32),
                pltpu.VMEM((4, 2 * BLOCK, 2 * HEAD_DIM), jnp.bfloat16),
                pltpu.VMEM((4, 2 * HEAD_DIM, 2 * BLOCK), jnp.bfloat16),
                pltpu.VMEM((blocks, HEAD_DIM, BLOCK), jnp.bfloat16),
            ],
        ),
        out_shape=[
            jax.ShapeDtypeStruct((kv_heads * wide, BLOCK), jnp.bfloat16),
            jax.ShapeDtypeStruct((kv_heads * wide, BLOCK), jnp.bfloat16),
            jax.ShapeDtypeStruct((chips, 2, 2 * BLOCK, kv_heads * HEAD_DIM), jnp.bfloat16),
            jax.ShapeDtypeStruct((kv_heads * GROUP, BLOCK), jnp.float32),
        ],
        compiler_params=pltpu.CompilerParams(vmem_limit_bytes=58 * 2**20),
        cost_estimate=pl.CostEstimate(
            flops=2 * 10 * pairs * BLOCK * KB * BLOCK * HEAD_DIM,
            bytes_accessed=2 * 2 * chips * 2 * 2 * BLOCK * kv_heads * HEAD_DIM,
            transcendentals=pairs * BLOCK * KB * BLOCK,
        ),
    )(core, table, sink, q, q_other, g, g_other, q.T, q_other.T, g.T, g_other.T, kv, kv)


def shards(queries, key_states, value_states, sink_logit, out_grad, block_table):
    devices = lax.axis_size("seq")
    chips = devices // 2
    me = lax.axis_index("seq")
    chip, core = me // 2, me % 2
    half = HEADS // 2
    swap = lambda x: lax.ppermute(x, "seq", [(i, i ^ 1) for i in range(devices)])
    groups = [list(range(0, devices, 2)), list(range(1, devices, 2))]
    cut = lambda x, which, size: lax.dynamic_slice_in_dim(x, which * size, size, axis=x.ndim - 1)
    order = lambda mine, theirs: jnp.concatenate(
        [jnp.where(core == 0, mine, theirs), jnp.where(core == 0, theirs, mine)], -1
    )

    kv_all = lax.all_gather(jnp.concatenate([key_states, value_states], 2), "seq", axis=0, tiled=True)

    q_local, g_local = queries[0], out_grad[0]
    q_other = swap(cut(q_local, 1 - core, half * HEAD_DIM))
    g_other = swap(cut(g_local, 1 - core, half * HEAD_DIM))

    blocks = block_table.shape[1]
    info = jnp.concatenate(
        [
            block_table.astype(jnp.float32).reshape(blocks, KB),
            jnp.broadcast_to(sink_logit.reshape(1, 1), (blocks, 1)),
        ],
        1,
    ).reshape(chips, 1, 2 * (KB + 1))
    info = jnp.broadcast_to(info, (chips, 2, 2 * (KB + 1))).reshape(devices, 2 * (KB + 1))
    info = lax.all_to_all(info, "seq", split_axis=0, concat_axis=0, tiled=True)
    info = lax.dynamic_slice_in_dim(info, core * half, half, axis=0).reshape(half, 2, KB + 1)
    table = info[:, :, :KB].astype(jnp.int32)
    table = jnp.where(core == 0, table, table[:, ::-1])
    sink = info[:, 0, KB]
    core_at = core.reshape(1).astype(jnp.int32)
    local = (q_local, q_other, g_local, g_other)
    dq_own, dq_other, dkv, dsink = attention(
        core_at, table.reshape(-1), sink, *local, kv_all
    )
    dkv_chip = lax.psum_scatter(
        dkv, "seq", scatter_dimension=0, tiled=True, axis_index_groups=groups
    )[0]
    sides = (dkv_chip[:, :BLOCK], swap(dkv_chip[:, BLOCK:]))
    key_grad = order(*[x[0] for x in sides])[None]
    value_grad = order(*[x[1] for x in sides])[None]

    query_grad = order(dq_own.T, swap(dq_other).T)[None]

    total = jnp.sum(dsink, 1).reshape(1, half)
    for step in (1, 2, 4, 8):
        total += lax.ppermute(total, "dp", [(i, i ^ step) for i in range(16)])
    for step in (2, 4, 8, 16):
        total += lax.ppermute(total, "seq", [(i, i ^ step) for i in range(devices)])
    sinks = order(total, swap(total)).reshape(HEADS)
    sink_grad = lax.dynamic_slice_in_dim(sinks, me, 1)
    return (query_grad, key_grad, value_grad, sink_grad)


def solution(mesh):
    in_specs = (
        P("dp", "seq", None),
        P("dp", "seq", None),
        P("dp", "seq", None),
        P("seq"),
        P("dp", "seq", None),
        P("seq", None, None),
    )
    out_specs = (P("dp", "seq", None), P("dp", "seq", None), P("dp", "seq", None), P("seq"))
    return jax.shard_map(shards, mesh=mesh, in_specs=in_specs, out_specs=out_specs, check_vma=False)
```
